768 devices in a mesh: dp: 12 (over z), expert: 64 (over x, y, core).
Axes of the slice: x: 4, y: 8, z: 12, core: 2. Of those that a mesh axis runs over, the one named last changes fastest.
Arguments:
- cotangent: bfloat16 [98304, 7168], P(('dp', 'expert')), may hold values from -6 to 6
- logits: float32 [98304, 8], P(('dp', 'expert')), may hold values from -8 to 8
- group_pick: int32 [98304, 8], P(('dp', 'expert')), may hold values from 0 to 7, as said below
- member_pick: int32 [98304, 8], P(('dp', 'expert')), may hold values from 0 to 31, as said below
- saved_gate: bfloat16 [1536, 8192], P('dp', 'expert'), may hold values from -6 to 6
- saved_up: bfloat16 [1536, 8192], P('dp', 'expert'), may hold values from -6 to 6
- gate_weight: bfloat16 [7168, 8192], P(None, 'expert'), may hold values from -0.0625 to 0.0625
- up_weight: bfloat16 [7168, 8192], P(None, 'expert'), may hold values from -0.0625 to 0.0625
- down_weight: bfloat16 [8192, 7168], P('expert'), may hold values from -0.125 to 0.125
Outputs:
- token_grad: bfloat16 [98304, 7168], P(('dp', 'expert'))
- logit_grad: float32 [98304, 8], P(('dp', 'expert'))
- down_grad: bfloat16 [8192, 7168], P('expert')
The draws below stay inside these ranges and needn't reach their ends.
Inputs may be any that keep to these rules, and one draw needn't show every extreme that they name: Route k of token t goes to expert 32 * group_pick[t, k] + member_pick[t, k]; a token's 8 experts are distinct. Among the 128 tokens of one device no window expert is named more than 2 times, and one window expert is named exactly 2 times by the tokens of every device. `member_pick`: see group_pick.
All inputs are finite; a program needn't handle non-finite values.
Results may differ from the reference program's by a relative error of at most 0.02.
Values may be sent and summed in bfloat16 or wider, within the bound.
A program may use at most 64 MiB of HBM per device.

```python
import jax
import jax.numpy as jnp
from jax import lax

D = 7168
FF = 2048
EXPERTS_ALL = 256
TOP = 8
EXPERTS = 4
CAP = 2
TOK_DEV = 128
GROUP_SIZE = 32
STRIDE = 64
TOKENS = 98304
SLOTS = 1536
N_DP = 12
N_EXPERT = 64


def route_table(key):
    slot_total = TOK_DEV * TOP
    others = EXPERTS_ALL - EXPERTS
    places = EXPERTS * CAP
    blocks = N_DP * N_EXPERT
    hot_key, block_root = jax.random.split(jax.random.fold_in(key, 101))
    hot_owner = jax.random.randint(hot_key, (), 0, EXPERTS)
    expert_ids = jnp.arange(EXPERTS_ALL, dtype=jnp.int32)
    window_mask = expert_ids % STRIDE == 0

    def one_block(block_key):
        order_key, coin_key, row_key, column_key = jax.random.split(block_key, 4)
        order = jax.random.permutation(order_key, EXPERTS_ALL).astype(jnp.int32)
        score = jnp.where(window_mask, EXPERTS_ALL + expert_ids, order)
        ranked = jnp.argsort(score, stable=True).astype(jnp.int32)
        slot_index = jnp.arange(slot_total, dtype=jnp.int32)
        table = ranked[slot_index % others].reshape(TOK_DEV, TOP)
        place = jnp.arange(places, dtype=jnp.int32)
        owner = place // CAP
        coins = jax.random.randint(coin_key, (places,), 0, 2)
        used = (place % CAP == 0) | (owner == hot_owner) | (coins == 1)
        first = jnp.where(used, owner * STRIDE, table[:places, 0])
        table = table.at[:places, 0].set(first.astype(jnp.int32))
        table = table[jax.random.permutation(row_key, TOK_DEV)]
        table = jax.random.permutation(column_key, table, axis=1, independent=True)
        return table
    block_keys = jax.random.split(block_root, blocks)
    return jax.vmap(one_block)(block_keys).reshape(blocks * TOK_DEV, TOP).astype(jnp.int32)


def draw_group_pick(key, part):
    table = route_table(key)
    return (table // GROUP_SIZE).astype(jnp.int32)


def draw_member_pick(key, part):
    table = route_table(key)
    return (table % GROUP_SIZE).astype(jnp.int32)


def shard_levels(stream_key, dims, cuts, low, high):
    level, own = 1.0, jax.random.fold_in(stream_key, 6)
    for dim, shards_of in cuts:
        heights = jnp.exp(jax.random.uniform(jax.random.fold_in(own, dim), (shards_of,), jnp.float32, low / len(cuts), high / len(cuts)))
        level = level * jnp.repeat(heights, dims[dim] // shards_of).reshape([-1 if axis == dim else 1 for axis in range(len(dims))])
    return level


def scatter_about(rng, shape, spread, bound, cuts=(), kind=jnp.bfloat16):
    entries = spread * jax.random.normal(rng, shape, jnp.float32)
    if cuts:
        entries = entries * shard_levels(rng, shape, cuts, -0.22, 0.18)
    return jnp.clip(entries, -bound, bound).astype(kind)


def setup_inputs(seed: int = 0) -> dict:
    arg_keys = jax.random.split(jax.random.key(seed), 10)
    return {
        "cotangent": scatter_about(arg_keys[0], (TOKENS, D), 1.0, 6.0, ((0, 768),)),
        "logits": scatter_about(arg_keys[1], (TOKENS, TOP), 2.0, 8.0, ((0, 768),), jnp.float32),
        "group_pick": draw_group_pick(jax.random.fold_in(arg_keys[9], 71), 0),
        "member_pick": draw_member_pick(jax.random.fold_in(arg_keys[9], 71), 0),
        "saved_gate": scatter_about(arg_keys[4], (SLOTS, EXPERTS * FF), 1.0, 6.0, ((0, 12), (1, 64))),
        "saved_up": scatter_about(arg_keys[5], (SLOTS, EXPERTS * FF), 1.0, 6.0, ((0, 12), (1, 64))),
        "gate_weight": scatter_about(arg_keys[6], (D, EXPERTS * FF), D ** -0.5, 0.0625, ((1, 64),)),
        "up_weight": scatter_about(arg_keys[7], (D, EXPERTS * FF), D ** -0.5, 0.0625, ((1, 64),)),
        "down_weight": scatter_about(arg_keys[8], (EXPERTS * FF, D), FF ** -0.5, 0.125, ((0, 64),)),
    }


route_scale = 2.5
highest = lax.Precision.HIGHEST


def rounded(values):
    return lax.optimization_barrier(values.astype(jnp.bfloat16)).astype(jnp.float32)


def one_expert(gate_saved, up_saved, slot_grads, weighted, gate_cols, up_cols, down_rows):
    hidden_blocks = N_EXPERT // EXPERTS
    block_width = FF // hidden_blocks
    gate_pre = gate_saved.astype(jnp.float32)
    up_pre = up_saved.astype(jnp.float32)
    sigmoid_gate = jax.nn.sigmoid(gate_pre)
    activated = gate_pre * sigmoid_gate
    hidden = (activated * up_pre).astype(jnp.bfloat16)
    grad_hidden = jnp.dot(weighted, down_rows.T, preferred_element_type=jnp.float32)
    grad_gate = (grad_hidden * up_pre * sigmoid_gate * (1.0 + gate_pre * (1.0 - sigmoid_gate))).astype(jnp.bfloat16)
    grad_up = (grad_hidden * activated).astype(jnp.bfloat16)
    grads_wide = slot_grads.astype(jnp.float32)

    def per_block(carry, block_index):
        start = (block_index * block_width).astype(jnp.int32)
        hidden_part = lax.dynamic_slice_in_dim(hidden, start, block_width, 1)
        down_part = lax.dynamic_slice_in_dim(down_rows, start, block_width, 0)
        gate_part = lax.dynamic_slice_in_dim(gate_cols, start, block_width, 1)
        up_part = lax.dynamic_slice_in_dim(up_cols, start, block_width, 1)
        grad_gate_part = lax.dynamic_slice_in_dim(grad_gate, start, block_width, 1)
        grad_up_part = lax.dynamic_slice_in_dim(grad_up, start, block_width, 1)
        slice_out = rounded(jnp.dot(hidden_part, down_part, preferred_element_type=jnp.float32))
        router_term = rounded(jnp.sum(slice_out * grads_wide, axis=1))
        backward = jnp.dot(grad_gate_part, gate_part.T, preferred_element_type=jnp.float32)
        backward = backward + jnp.dot(grad_up_part, up_part.T, preferred_element_type=jnp.float32)
        return carry + rounded(backward), router_term

    grad_rows, router_terms = lax.scan(per_block, jnp.zeros(slot_grads.shape, jnp.float32), jnp.arange(hidden_blocks, dtype=jnp.int32))
    router_sum = jnp.sum(router_terms, axis=0)
    hidden_groups = hidden.reshape(N_DP, -1, FF)
    weighted_groups = weighted.reshape(N_DP, -1, D)

    def per_group(carry, pair):
        return carry + rounded(jnp.dot(pair[0].T, pair[1], preferred_element_type=jnp.float32)), None

    down_sum, unused = lax.scan(per_group, jnp.zeros((FF, D), jnp.float32), (hidden_groups, weighted_groups))
    return grad_rows, router_sum, down_sum.astype(jnp.bfloat16)


def reference(cotangent, logits, group_pick, member_pick, saved_gate, saved_up, gate_weight, up_weight, down_weight):
    blocks = N_DP * N_EXPERT
    chosen = (group_pick * GROUP_SIZE + member_pick).reshape(blocks, TOK_DEV, TOP)
    window_ids = jnp.arange(EXPERTS, dtype=jnp.int32) * STRIDE
    route_hits = (chosen[..., None] == window_ids[None, None, None, :]).astype(jnp.float32)
    in_window = jnp.sum(route_hits, axis=2)
    earlier = jnp.cumsum(in_window, axis=1) - in_window
    slot_numbers = jnp.arange(CAP, dtype=jnp.float32)
    window_first = jnp.transpose(in_window, (0, 2, 1))[:, :, None, :]
    earlier_first = jnp.transpose(earlier, (0, 2, 1))[:, :, None, :]
    slot_map = window_first * (earlier_first == slot_numbers[None, None, :, None]).astype(jnp.float32)
    affinity = jax.nn.sigmoid(logits).reshape(blocks, TOK_DEV, TOP)
    affinity_sum = jnp.sum(affinity, axis=2, keepdims=True)
    gate_value = rounded(route_scale * affinity / affinity_sum)
    window_gate = jnp.einsum("btke,btk->bte", route_hits, gate_value, precision=highest)
    slot_gate = jnp.einsum("bect,bte->ebc", slot_map, window_gate, precision=highest)
    grad_blocks = cotangent.reshape(blocks, TOK_DEV, D).astype(jnp.float32)
    slot_grads = jnp.einsum("bect,btd->ebcd", slot_map, grad_blocks, precision=highest).astype(jnp.bfloat16)
    weighted = (slot_gate[..., None] * slot_grads.astype(jnp.float32)).astype(jnp.bfloat16)
    grad_pieces = []
    router_pieces = []
    down_pieces = []
    for expert in range(EXPERTS):
        low = expert * FF
        grad_rows, router_sum, down_block = one_expert(
            saved_gate[:, low:low + FF],
            saved_up[:, low:low + FF],
            slot_grads[expert].reshape(-1, D),
            weighted[expert].reshape(-1, D),
            gate_weight[:, low:low + FF],
            up_weight[:, low:low + FF],
            down_weight[low:low + FF, :],
        )
        grad_pieces.append(grad_rows.reshape(blocks, CAP, D))
        router_pieces.append(router_sum.reshape(blocks, CAP))
        down_pieces.append(down_block)
    grad_slot = jnp.stack(grad_pieces)
    router_slot = jnp.stack(router_pieces)
    token_grad = jnp.einsum("bect,ebcd->btd", slot_map, grad_slot, precision=highest)
    token_grad = token_grad.reshape(TOKENS, D).astype(jnp.bfloat16)
    window_grad = jnp.einsum("bect,ebc->bte", slot_map, router_slot, precision=highest)
    route_grad = jnp.einsum("btke,bte->btk", route_hits, window_grad, precision=highest)
    spread_mean = jnp.sum(route_grad * affinity, axis=2, keepdims=True) / affinity_sum
    logit_grad = affinity * (1.0 - affinity) * route_scale / affinity_sum * (route_grad - spread_mean)
    down_grad = jnp.concatenate(down_pieces, axis=0)
    return token_grad, logit_grad.reshape(TOKENS, TOP), down_grad
```

```python
import functools

import jax
import jax.numpy as jnp
from jax import lax
from jax.experimental import pallas as pl
from jax.experimental.pallas import tpu as pltpu
from jax.sharding import PartitionSpec as P

EXPERTS = 4
CAP = 2
GROUP_SIZE = 32
STRIDE = 64
route_scale = 2.5
MESH = pl.DeviceIdType.MESH
bf16 = jnp.bfloat16
f32 = jnp.float32

NX = EXPERTS
NY = 8
NZ = 12
SPAN = 640


def iota(shape, dim):
    return lax.broadcasted_iota(jnp.int32, shape, dim)


def one_hot(mask):
    return jnp.where(mask, 1.0, 0.0).astype(bf16)


def mm(a, b, ca=1, cb=0):
    return lax.dot_general(a, b, (((ca,), (cb,)), ((), ())), preferred_element_type=f32)


def split(v):
    hi = v.astype(bf16)
    rest = v - hi.astype(f32)
    mid = rest.astype(bf16)
    low = (rest - mid.astype(f32)).astype(bf16)
    return hi, mid, low


def routing(logits, group, member):
    chosen = group * GROUP_SIZE + member
    affinity = jax.nn.sigmoid(logits)
    affinity_sum = jnp.sum(affinity, axis=0, keepdims=True)
    gate = (route_scale * affinity / affinity_sum).astype(bf16).astype(f32)
    row = iota(chosen.shape, 0)
    hits = [chosen == w * STRIDE for w in range(EXPERTS)]
    member8 = jnp.zeros(chosen.shape, f32)
    gate8 = jnp.zeros(chosen.shape, f32)
    for w in range(EXPERTS):
        in_window = jnp.sum(jnp.where(hits[w], 1.0, 0.0), axis=0, keepdims=True)
        window_gate = jnp.sum(jnp.where(hits[w], gate, 0.0), axis=0, keepdims=True)
        mine = (row // CAP) == w
        member8 = jnp.where(mine, in_window, member8)
        gate8 = jnp.where(mine, window_gate, gate8)
    tokens = chosen.shape[1]
    before = one_hot(iota((tokens, tokens), 0) < iota((tokens, tokens), 1))
    earlier = mm(member8.astype(bf16), before)
    slot8 = jnp.where(earlier == (row % CAP).astype(f32), member8, 0.0)
    return affinity, affinity_sum, hits, slot8, gate8


def expand_rows(rows):
    i = iota((rows, EXPERTS * CAP), 0)
    j = iota((rows, EXPERTS * CAP), 1)
    per = rows // EXPERTS
    return one_hot((i // per) * CAP + i % CAP == j)


def main_kernel(
    logits_ref, group_ref, member_ref, sg_ref, su_ref, cot_hbm, gate_hbm, up_hbm, down_hbm,
    yr, dg,
    cotv, downv, guv, xs, xr, av, w2, hv, gp, upv, own, qs, qr, p0, p1, sm0, sm1, rm0, rm1, ys,
    load_sem,
    xs_s, xs_r, za_s, za_r, a_s, a_r, as_s, as_r, b_s, b_r, bs_s, bs_r, h_s, h_r, o_s, o_r,
    q_s, q_r, m_s, m_r, y_s, y_r, loc,
):
    e = lax.axis_index("expert")
    z = lax.axis_index("dp")
    x = e // (2 * NY)
    y = (e // 2) % NY
    c = e % 2
    other = 1 - c
    half = cotv.shape[0] // 2
    seg = cotv.shape[2]
    subw = seg * 2
    pending = []

    def at(zz, xx, yy, cc):
        return (zz, (xx * NY + yy) * 2 + cc)

    def send(src, dst, ssem, rsem, dev):
        copy = pltpu.make_async_remote_copy(
            src_ref=src, dst_ref=dst, send_sem=ssem, recv_sem=rsem, device_id=dev, device_id_type=MESH
        )
        copy.start()
        pending.append(copy)

    def arrived(dst, rsem):
        pltpu.make_async_remote_copy(
            src_ref=dst, dst_ref=dst, send_sem=rsem, recv_sem=rsem,
            device_id=at(z, x, y, other), device_id_type=MESH,
        ).wait_recv()

    loads = []

    def load(src, dst, k):
        copy = pltpu.make_async_copy(src, dst, load_sem.at[k])
        copy.start()
        loads.append(copy)

    for j in range(8):
        load(cot_hbm.at[:, pl.ds(j * seg, seg)], cotv.at[j], j)
    for j in range(4):
        load(down_hbm.at[:, pl.ds(j * subw, subw)], downv.at[j], 8 + j)
    for j in range(8):
        load(gate_hbm.at[pl.ds(j * seg, seg), :], guv.at[j, :, pl.ds(0, 128)], 12 + j)
        load(up_hbm.at[pl.ds(j * seg, seg), :], guv.at[j, :, pl.ds(128, 128)], 20 + j)

    barrier = pltpu.get_barrier_semaphore()
    greeted = 0

    def greet(dev):
        pl.semaphore_signal(barrier, inc=1, device_id=dev, device_id_type=MESH)

    for dz in range(NZ):
        for dc in range(2):
            if dz or dc:
                greet(at((z + dz) % NZ, x, y, (c + dc) % 2))
                greeted += 1
    for dx in range(1, NX):
        for dc in range(2):
            greet(at(z, (x + dx) % NX, y, (c + dc) % 2))
            greeted += 1
    for dy in (1, NY - 1):
        greet(at(z, x, (y + dy) % NY, c))
        greeted += 1

    def own_hidden():
        i = iota((128, 128), 0)
        k = iota((128, 128), 1)
        perm = one_hot(k == ((i // 4) % NX) * (4 * NY) + (i // (4 * NX)) * 4 + i % 4)
        gp[...] = mm(perm, sg_ref[...])
        upv[...] = mm(perm, su_ref[...])
        gate_pre = gp[...]
        hidden = (gate_pre * jax.nn.sigmoid(gate_pre) * upv[...]).astype(bf16)
        zz = z // 2
        hv[z % 2, zz // 3, :, zz % 3] = hidden.reshape(NY, 16, 128)

    own_hidden()

    affinity, affinity_sum, hits, slot8, gate8 = routing(logits_ref[...], group_ref[...], member_ref[...])
    rows64 = mm(expand_rows(64), (slot8 * gate8).astype(bf16))
    rowseg = (iota((64, 128), 0) // CAP) % 8
    spread = jnp.concatenate(
        [jnp.where(rowseg == j, rows64, 0.0).astype(bf16) for j in range(8)], axis=1
    )
    for j in range(8):
        loads[j].wait()
    gated = mm(spread, cotv[...].reshape(8 * 128, seg))
    xs[...] = gated.reshape(NX, 2, 8, seg)

    pl.semaphore_wait(barrier, greeted)

    h_steps = [(0, t) for t in range(NZ // 2)] + [(1, t) for t in range(NZ // 2 - 1)]

    def hchunk(zz):
        return hv.at[zz % 2, (zz // 2) // 3, :, (zz // 2) % 3]

    def h_send(d, t):
        s = 1 if d == 0 else -1
        ref = hchunk((z - s * t + NZ) % NZ)
        k = d * (NZ // 2) + t
        send(ref, ref, h_s.at[k], h_r.at[k], at((z + s + NZ) % NZ, x, y, c))

    def h_recv(d, t):
        s = 1 if d == 0 else -1
        arrived(hchunk((z - s * (t + 1) + NZ) % NZ), h_r.at[d * (NZ // 2) + t])
        if (d, t + 1) in h_steps:
            h_send(d, t + 1)

    keep = pltpu.make_async_copy(xs.at[x, c], xr.at[x, c], xs_r.at[x * 2 + c])
    for dx in range(NX):
        for dc in range(2):
            if dx == 0 and dc == 0:
                keep.start()
                continue
            xx, cc = (x + dx) % NX, (c + dc) % 2
            send(xs.at[xx, cc], xr.at[x, c], xs_s.at[dx * 2 + dc], xs_r.at[x * 2 + c], at(z, xx, y, cc))
    h_send(0, 0)
    h_send(1, 0)
    for xx in range(NX):
        for cc in range(2):
            arrived(xr.at[xx, cc], xs_r.at[xx * 2 + cc])
    i16 = iota((16, 64), 0)
    k16 = iota((16, 64), 1)
    got = xr[...].reshape(64, seg).astype(bf16)
    for s in range(4):
        pick = one_hot(((k16 // 8) * CAP + k16 % CAP == i16) & ((k16 // CAP) % 4 == s))
        av[c, s // 2, y, :, pl.ds((s % 2) * seg, seg)] = mm(pick, got).astype(bf16)

    def ring(buf, ssem, rsem, sib_s, sib_r):
        steps = {(d, s): (NY // 2 if d == s else NY // 2 - 1) for d in range(2) for s in range(2)}

        def number(d, s, t):
            return (d * 2 + s) * (NY // 2) + t

        def put(d, s, t):
            g = 1 if d == 0 else -1
            ref = buf.at[c, s, (y - g * t + NY) % NY]
            k = number(d, s, t)
            send(ref, ref, ssem.at[k], rsem.at[k], at(z, x, (y + g + NY) % NY, c))

        def across(yy, s, k):
            ref = buf.at[c, s, yy]
            send(ref, ref, sib_s.at[k], sib_r.at[k], at(z, x, y, other))

        def first():
            for s in range(2):
                put(0, s, 0)
                put(1, s, 0)
            for s in range(2):
                across(y, s, 16 + s)

        def turn(t):
            for s in range(2):
                for d in range(2):
                    if t < steps[d, s]:
                        g = 1 if d == 0 else -1
                        yy = (y - g * (t + 1) + NY) % NY
                        k = number(d, s, t)
                        arrived(buf.at[c, s, yy], rsem.at[k])
                        if t + 1 < steps[d, s]:
                            put(d, s, t + 1)
                        across(yy, s, k)

        def last():
            for s in range(2):
                arrived(buf.at[other, s, y], sib_r.at[16 + s])
                for d in range(2):
                    g = 1 if d == 0 else -1
                    for t in range(steps[d, s]):
                        yy = (y - g * (t + 1) + NY) % NY
                        arrived(buf.at[other, s, yy], sib_r.at[number(d, s, t)])

        return first, turn, last

    a_first, a_turn, a_last = ring(av, a_s, a_r, as_s, as_r)
    b_first, b_turn, b_last = ring(w2, b_s, b_r, bs_s, bs_r)
    a_first()

    def first_tile(k):
        return (14 * k) // 3

    zq = z // 2
    per_half = NZ // 2
    for k in range(per_half):
        zz = c * per_half + k
        start = first_tile(k) * 128
        src = av.at[c, start // subw, y, :, pl.ds(start % subw, SPAN)]
        dst = w2.at[z % 2, zq // 3, y, zq % 3]
        copy = pltpu.make_async_remote_copy(
            src_ref=src, dst_ref=dst, send_sem=za_s.at[k], recv_sem=za_r.at[zq],
            device_id=at(zz, x, y, z % 2), device_id_type=MESH,
        )
        here = pltpu.make_async_copy(src, dst, za_r.at[zq])
        remote = jnp.logical_or(zz != z, z % 2 != c)

        @pl.when(remote)
        def _(copy=copy):
            copy.start()

        @pl.when(jnp.logical_not(remote))
        def _(here=here):
            here.start()
        pending.append((copy, remote))
    for q in range(NZ // 2):
        arrived(w2.at[c, q // 3, y, q % 3], za_r.at[q])
    b_first()

    for t in range(NY // 2):
        a_turn(t)
        b_turn(t)
        for k in (t * 2, t * 2 + 1):
            for d in range(2):
                if (d, k) in h_steps:
                    h_recv(d, k)
    b_last()

    mine = mm(hv[...].reshape(-1, 128), w2[...].reshape(-1, SPAN), 0, 0).astype(bf16)
    own[...] = mine.reshape(2, 64, SPAN)
    keep_out = pltpu.make_async_copy(own, dg.at[z], loc.at[0])
    keep_out.start()
    o_steps = {(d, s): (NZ // 2 if d == s else NZ // 2 - 1) for d in range(2) for s in range(2)}

    def o_send(d, s, t):
        g = 1 if d == 0 else -1
        zz = (z - g * t + NZ) % NZ
        k = (d * 2 + s) * (NZ // 2) + t
        src = own.at[s] if t == 0 else dg.at[zz, s]
        send(src, dg.at[zz, s], o_s.at[k], o_r.at[k], at((z + g + NZ) % NZ, x, y, c))

    def o_turn(t):
        for s in range(2):
            for d in range(2):
                if t < o_steps[d, s]:
                    g = 1 if d == 0 else -1
                    k = (d * 2 + s) * (NZ // 2) + t
                    arrived(dg.at[(z - g * (t + 1) + NZ) % NZ, s], o_r.at[k])
                    if t + 1 < o_steps[d, s]:
                        o_send(d, s, t + 1)

    for s in range(2):
        o_send(0, s, 0)
        o_send(1, s, 0)

    a_last()
    for j in range(8, 28):
        loads[j].wait()
    grad_hidden = mm(av[0, 0].reshape(128, subw), downv[0], 1, 1)
    for j in range(1, 4):
        grad_hidden += mm(av[j // 2, j % 2].reshape(128, subw), downv[j], 1, 1)
    gate_pre = gp[...]
    up_pre = upv[...]
    sig = jax.nn.sigmoid(gate_pre)
    act = gate_pre * sig
    hidden = (act * up_pre).astype(bf16).astype(f32)
    p1[:, :, pl.ds(subw, 128)] = (hidden * grad_hidden).reshape(NY, 16, 128)
    grad_gate = (grad_hidden * up_pre * sig * (1.0 + gate_pre * (1.0 - sig))).astype(bf16)
    grad_up = (grad_hidden * act).astype(bf16)
    both = jnp.concatenate([grad_gate, grad_up], axis=1)
    for s in range(4):
        qs[s] = mm(both, guv[other * 4 + s], 1, 1).astype(bf16)
        send(qs.at[s], qr.at[s], q_s.at[s], q_r.at[s], at(z, x, y, other))
    for s in range(4):
        part = mm(both, guv[c * 4 + s], 1, 1)
        (p0, p1)[s // 2][:, :, pl.ds((s % 2) * seg, seg)] = part.reshape(NY, 16, seg)

    pp, sm, rm = (p0, p1), (sm0, sm1), (rm0, rm1)
    m_steps = {(d, s): (NY // 2 if d == s else NY // 2 - 1) for d in range(2) for s in range(2)}

    def m_number(d, t):
        return d * (NY // 2) + t

    def m_send(d, s, t):
        g = 1 if d == 0 else -1
        left = m_steps[d, s] - t
        value = pp[s][(y + g * left + NY) % NY]
        n = m_number(d, t)
        if t:
            value = value + rm[s][m_number(d, t - 1)].astype(f32)
        sm[s][n] = value.astype(bf16)
        send(sm[s].at[n], rm[s].at[n], m_s.at[s * 8 + n], m_r.at[s * 8 + n], at(z, x, (y + g + NY) % NY, c))

    for s in range(4):
        arrived(qr.at[s], q_r.at[s])
        ref = (p0, p1)[s // 2]
        cols = pl.ds((s % 2) * seg, seg)
        ref[:, :, cols] = ref[:, :, cols] + qr[s].astype(f32).reshape(NY, 16, seg)
        if s % 2:
            m_send(0, s // 2, 0)
            m_send(1, s // 2, 0)
    for t in range(NY // 2):
        for s in range(2):
            for d in range(2):
                if t < m_steps[d, s]:
                    n = m_number(d, t)
                    arrived(rm[s].at[n], m_r.at[s * 8 + n])
                    if t + 1 < m_steps[d, s]:
                        m_send(d, s, t + 1)
        o_turn(t)

    i64 = iota((64, 16), 0)
    k64 = iota((64, 16), 1)
    totals = []
    for s in range(2):
        total = pp[s][y]
        for d in range(2):
            total = total + rm[s][m_number(d, m_steps[d, s] - 1)].astype(f32)
        totals.append(total)
    out = jnp.zeros((64, seg), f32)
    source = (i64 // 8) * CAP + i64 % CAP
    for s in range(4):
        pick = one_hot((source == k64) & ((i64 // CAP) % 4 == s))
        for piece in split(totals[s // 2][:, (s % 2) * seg:(s % 2) * seg + seg]):
            out = out + mm(pick, piece)
    products = jnp.zeros((64, 128), f32)
    pick = one_hot((source == k64) & ((i64 // CAP) % 4 == 0))
    for piece in split(totals[1][:, subw:subw + 128]):
        products = products + mm(pick, piece)
    ys[:, :, :, pl.ds(0, seg)] = out.reshape(NX, 2, 8, seg)
    ys[:, :, :, pl.ds(seg, 128)] = products.reshape(NX, 2, 8, 128)
    keep = pltpu.make_async_copy(ys.at[x, c], yr.at[x, c], y_r.at[x * 2 + c])
    for dx in range(NX):
        for dc in range(2):
            if dx == 0 and dc == 0:
                keep.start()
                continue
            xx, cc = (x + dx) % NX, (c + dc) % 2
            send(ys.at[xx, cc], yr.at[x, c], y_s.at[dx * 2 + dc], y_r.at[x * 2 + c], at(z, xx, y, cc))
    for t in range(NY // 2, NZ // 2):
        o_turn(t)
    for xx in range(NX):
        for cc in range(2):
            arrived(yr.at[xx, cc], y_r.at[xx * 2 + cc])
    keep_out.wait()
    for item in pending:
        if isinstance(item, tuple):
            copy, cond = item

            @pl.when(cond)
            def _(copy=copy):
                copy.wait_send()
        else:
            item.wait_send()


def final_kernel(
    logits_ref, group_ref, member_ref, yr_ref, dg, token_out, logit_ref, down_out, stage, sems
):
    seg = stage.shape[2]
    per_half = NZ // 2
    copies = []
    for zz in range(NZ):
        k = zz % per_half
        start = (14 * k) // 3
        width = ((14 * (k + 1)) // 3 - start) * 128
        start = (zz // per_half) * 4 * seg + start * 128
        for s in range(2):
            copy = pltpu.make_async_copy(
                dg.at[zz, s, :, pl.ds(0, width)],
                down_out.at[pl.ds(s * 64, 64), pl.ds(start, width)],
                sems.at[8 + zz * 2 + s],
            )
            copy.start()
            copies.append(copy)
    affinity, affinity_sum, hits, slot8, gate8 = routing(logits_ref[...], group_ref[...], member_ref[...])
    grads = yr_ref[:, :, :, 0:seg].reshape(64, seg)
    pieces = jnp.concatenate(split(grads), axis=0)
    expand = expand_rows(64)
    place = mm(slot8.astype(bf16), expand, 0, 1)
    colseg = (iota((128, 64), 1) // CAP) % 8
    for j in range(8):
        chosen = jnp.where(colseg == j, place, 0.0).astype(bf16)
        stage[j] = mm(jnp.concatenate([chosen] * 3, axis=1), pieces).astype(bf16)
        copy = pltpu.make_async_copy(stage.at[j], token_out.at[:, pl.ds(j * seg, seg)], sems.at[j])
        copy.start()
        copies.append(copy)
    products = yr_ref[:, :, :, seg:seg + 128].reshape(64, 128)
    folded = jnp.zeros((8, 128), f32)
    for piece in split(products):
        folded = folded + mm(expand, piece, 0, 0)
    router = jnp.sum(folded, axis=1, keepdims=True)
    used = slot8 > 0.0
    routes = jnp.where(used, router / jnp.where(used, gate8, 1.0), 0.0)
    row = iota(slot8.shape, 0)
    route_grad = jnp.zeros(slot8.shape, f32)
    for w in range(EXPERTS):
        window_grad = jnp.sum(jnp.where((row // CAP) == w, routes, 0.0), axis=0, keepdims=True)
        route_grad = jnp.where(hits[w], window_grad, route_grad)
    mean = jnp.sum(route_grad * affinity, axis=0, keepdims=True) / affinity_sum
    logit_ref[...] = affinity * (1.0 - affinity) * route_scale / affinity_sum * (route_grad - mean)
    for copy in copies:
        copy.wait()


def body(cotangent, logits, group_pick, member_pick, saved_gate, saved_up, gate_weight, up_weight, down_weight):
    tokens, width = cotangent.shape
    seg = width // 8
    subw = 2 * seg
    vmem = pl.BlockSpec(memory_space=pltpu.VMEM)
    hbm = pl.BlockSpec(memory_space=pl.ANY)
    logits_t, group_t, member_t = logits.T, group_pick.T, member_pick.T
    dma = pltpu.SemaphoreType.DMA
    scratch = [
        pltpu.VMEM((8, tokens, seg), bf16),
        pltpu.VMEM((4, 128, subw), bf16),
        pltpu.VMEM((8, seg, 256), bf16),
        pltpu.VMEM((NX, 2, 8, seg), f32),
        pltpu.VMEM((NX, 2, 8, seg), f32),
        pltpu.VMEM((2, 2, NY, 16, subw), bf16),
        pltpu.VMEM((2, 2, NY, 3, 16, SPAN), bf16),
        pltpu.VMEM((2, 2, NY, 3, 16, 128), bf16),
        pltpu.VMEM((128, 128), f32),
        pltpu.VMEM((128, 128), f32),
        pltpu.VMEM((2, 64, SPAN), bf16),
        pltpu.VMEM((4, 128, seg), bf16),
        pltpu.VMEM((4, 128, seg), bf16),
        pltpu.VMEM((NY, 16, subw), f32),
        pltpu.VMEM((NY, 16, subw + 128), f32),
        pltpu.VMEM((8, 16, subw), bf16),
        pltpu.VMEM((8, 16, subw + 128), bf16),
        pltpu.VMEM((8, 16, subw), bf16),
        pltpu.VMEM((8, 16, subw + 128), bf16),
        pltpu.VMEM((NX, 2, 8, seg + 128), f32),
        dma((28,)),
        dma((8,)), dma((8,)),
        dma((6,)), dma((6,)),
        dma((16,)), dma((16,)), dma((18,)), dma((18,)),
        dma((16,)), dma((16,)), dma((18,)), dma((18,)),
        dma((12,)), dma((12,)),
        dma((24,)), dma((24,)),
        dma((4,)), dma((4,)),
        dma((16,)), dma((16,)),
        dma((8,)), dma((8,)),
        dma((1,)),
    ]
    yr, dg = pl.pallas_call(
        main_kernel,
        out_shape=(
            jax.ShapeDtypeStruct((NX, 2, 8, seg + 128), f32),
            jax.ShapeDtypeStruct((NZ, 2, 64, SPAN), bf16),
        ),
        in_specs=[vmem] * 5 + [hbm] * 4,
        out_specs=(hbm, hbm),
        scratch_shapes=scratch,
        compiler_params=pltpu.CompilerParams(
            collective_id=0, has_side_effects=True, vmem_limit_bytes=62 * 1024 * 1024
        ),
    )(logits_t, group_t, member_t, saved_gate, saved_up, cotangent, gate_weight, up_weight, down_weight)
    token_grad, logit_grad, down_grad = pl.pallas_call(
        final_kernel,
        out_shape=(
            jax.ShapeDtypeStruct((tokens, width), bf16),
            jax.ShapeDtypeStruct((8, tokens), f32),
            jax.ShapeDtypeStruct((128, width), bf16),
        ),
        in_specs=[vmem] * 4 + [hbm],
        out_specs=(hbm, vmem, hbm),
        scratch_shapes=[pltpu.VMEM((8, tokens, seg), bf16), dma((32,))],
        compiler_params=pltpu.CompilerParams(vmem_limit_bytes=62 * 1024 * 1024),
    )(logits_t, group_t, member_t, yr, dg)
    return token_grad, logit_grad.T, down_grad


def solution(mesh):
    placed = (
        P(("dp", "expert"), None),
        P(("dp", "expert"), None),
        P(("dp", "expert"), None),
        P(("dp", "expert"), None),
        P("dp", "expert"),
        P("dp", "expert"),
        P(None, "expert"),
        P(None, "expert"),
        P("expert", None),
    )
    return jax.shard_map(
        body,
        mesh=mesh,
        in_specs=placed,
        out_specs=(P(("dp", "expert"), None), P(("dp", "expert"), None), P("expert", None)),
        check_vma=False,
    )
```

```python
import functools

import jax
import jax.numpy as jnp
from jax import lax
from jax.experimental import pallas as pl
from jax.experimental.pallas import tpu as pltpu
from jax.sharding import PartitionSpec as P

EXPERTS = 4
CAP = 2
GROUP_SIZE = 32
STRIDE = 64
route_scale = 2.5
MESH = pl.DeviceIdType.MESH
bf16 = jnp.bfloat16
f32 = jnp.float32

NX = EXPERTS
NY = 8
NZ = 12
SPANS = (384, 256)


def iota(shape, dim):
    return lax.broadcasted_iota(jnp.int32, shape, dim)


def one_hot(mask):
    return jnp.where(mask, 1.0, 0.0).astype(bf16)


def mm(a, b, ca=1, cb=0):
    return lax.dot_general(a, b, (((ca,), (cb,)), ((), ())), preferred_element_type=f32)


def split(v):
    hi = v.astype(bf16)
    rest = v - hi.astype(f32)
    mid = rest.astype(bf16)
    low = (rest - mid.astype(f32)).astype(bf16)
    return hi, mid, low


def routing(logits, group, member):
    chosen = group * GROUP_SIZE + member
    affinity = jax.nn.sigmoid(logits)
    affinity_sum = jnp.sum(affinity, axis=0, keepdims=True)
    gate = (route_scale * affinity / affinity_sum).astype(bf16).astype(f32)
    row = iota(chosen.shape, 0)
    hits = [chosen == w * STRIDE for w in range(EXPERTS)]
    member8 = jnp.zeros(chosen.shape, f32)
    gate8 = jnp.zeros(chosen.shape, f32)
    for w in range(EXPERTS):
        in_window = jnp.sum(jnp.where(hits[w], 1.0, 0.0), axis=0, keepdims=True)
        window_gate = jnp.sum(jnp.where(hits[w], gate, 0.0), axis=0, keepdims=True)
        mine = (row // CAP) == w
        member8 = jnp.where(mine, in_window, member8)
        gate8 = jnp.where(mine, window_gate, gate8)
    tokens = chosen.shape[1]
    before = one_hot(iota((tokens, tokens), 0) < iota((tokens, tokens), 1))
    earlier = mm(member8.astype(bf16), before)
    slot8 = jnp.where(earlier == (row % CAP).astype(f32), member8, 0.0)
    return affinity, affinity_sum, hits, slot8, gate8


def expand_rows(rows):
    i = iota((rows, EXPERTS * CAP), 0)
    j = iota((rows, EXPERTS * CAP), 1)
    per = rows // EXPERTS
    return one_hot((i // per) * CAP + i % CAP == j)


def main_kernel(
    logits_ref, group_ref, member_ref, sg_ref, su_ref, cot_hbm, gate_hbm, up_hbm, down_hbm,
    yr, dg0, dg1,
    cotv, downv, guv, xs, xr, av, w20, w21, hv, gp, upv, own0, own1, qs, qr, p0, p1, sm0, sm1, rm0, rm1, ys,
    load_sem,
    xs_s, xs_r, za_s, za_r, a_s, a_r, as_s, as_r, b_s, b_r, bs_s, bs_r, c_s, c_r, cs_s, cs_r, h_s, h_r, o_s, o_r,
    q_s, q_r, m_s, m_r, y_s, y_r, loc,
):
    e = lax.axis_index("expert")
    z = lax.axis_index("dp")
    x = e // (2 * NY)
    y = (e // 2) % NY
    c = e % 2
    other = 1 - c
    half = cotv.shape[0] // 2
    seg = cotv.shape[2]
    subw = seg * 2
    pending = []

    def at(zz, xx, yy, cc):
        return (zz, (xx * NY + yy) * 2 + cc)

    def send(src, dst, ssem, rsem, dev):
        copy = pltpu.make_async_remote_copy(
            src_ref=src, dst_ref=dst, send_sem=ssem, recv_sem=rsem, device_id=dev, device_id_type=MESH
        )
        copy.start()
        pending.append(copy)

    def arrived(dst, rsem):
        pltpu.make_async_remote_copy(
            src_ref=dst, dst_ref=dst, send_sem=rsem, recv_sem=rsem,
            device_id=at(z, x, y, other), device_id_type=MESH,
        ).wait_recv()

    loads = []

    def load(src, dst, k):
        copy = pltpu.make_async_copy(src, dst, load_sem.at[k])
        copy.start()
        loads.append(copy)

    for j in range(8):
        load(cot_hbm.at[:, pl.ds(j * seg, seg)], cotv.at[j], j)
    barrier = pltpu.get_barrier_semaphore()
    greeted = 0

    def greet(dev):
        pl.semaphore_signal(barrier, inc=1, device_id=dev, device_id_type=MESH)

    for dz in range(NZ):
        for dc in range(2):
            if dz or dc:
                greet(at((z + dz) % NZ, x, y, (c + dc) % 2))
                greeted += 1
    for dx in range(1, NX):
        for dc in range(2):
            greet(at(z, (x + dx) % NX, y, (c + dc) % 2))
            greeted += 1
    for dy in (1, NY - 1):
        greet(at(z, x, (y + dy) % NY, c))
        greeted += 1

    def own_hidden():
        i = iota((128, 128), 0)
        k = iota((128, 128), 1)
        perm = one_hot(k == ((i // 4) % NX) * (4 * NY) + (i // (4 * NX)) * 4 + i % 4)
        gp[...] = mm(perm, sg_ref[...])
        upv[...] = mm(perm, su_ref[...])
        gate_pre = gp[...]
        hidden = (gate_pre * jax.nn.sigmoid(gate_pre) * upv[...]).astype(bf16)
        zz = z // 2
        hv[z % 2, :, zz] = hidden.reshape(NY, 16, 128)

    affinity, affinity_sum, hits, slot8, gate8 = routing(logits_ref[...], group_ref[...], member_ref[...])
    rows64 = mm(expand_rows(64), (slot8 * gate8).astype(bf16))
    rowseg = (iota((64, 128), 0) // CAP) % 8
    spread = jnp.concatenate(
        [jnp.where(rowseg == j, rows64, 0.0).astype(bf16) for j in range(8)], axis=1
    )
    for j in range(8):
        loads[j].wait()
    gated = mm(spread, cotv[...].reshape(8 * 128, seg))
    xs[...] = gated.reshape(NX, 2, 8, seg)

    pl.semaphore_wait(barrier, greeted)

    keep = pltpu.make_async_copy(xs.at[x, c], xr.at[x, c], xs_r.at[x * 2 + c])
    for dx in (2, 1, 3, 0):
        for dc in range(2):
            if dx == 0 and dc == 0:
                keep.start()
                continue
            xx, cc = (x + dx) % NX, (c + dc) % 2
            send(xs.at[xx, cc], xr.at[x, c], xs_s.at[dx * 2 + dc], xs_r.at[x * 2 + c], at(z, xx, y, cc))
    for j in range(4):
        load(down_hbm.at[:, pl.ds(j * subw, subw)], downv.at[j], 8 + j)
    for j in range(8):
        load(gate_hbm.at[pl.ds(j * seg, seg), :], guv.at[j, :, pl.ds(0, 128)], 12 + j)
        load(up_hbm.at[pl.ds(j * seg, seg), :], guv.at[j, :, pl.ds(128, 128)], 20 + j)
    own_hidden()
    for xx in range(NX):
        for cc in range(2):
            arrived(xr.at[xx, cc], xs_r.at[xx * 2 + cc])
    i16 = iota((16, 64), 0)
    k16 = iota((16, 64), 1)
    got = xr[...].reshape(64, seg).astype(bf16)
    for s in range(4):
        pick = one_hot(((k16 // 8) * CAP + k16 % CAP == i16) & ((k16 // CAP) % 4 == s))
        av[c, s // 2, y, :, pl.ds((s % 2) * seg, seg)] = mm(pick, got).astype(bf16)

    def ring(chunk, longer, ssem, rsem, sib_s, sib_r):
        steps = [NY // 2 if d == longer else NY // 2 - 1 for d in range(2)]

        def put(d, t):
            g = 1 if d == 0 else -1
            ref = chunk(c, (y - g * t + NY) % NY)
            k = d * (NY // 2) + t
            send(ref, ref, ssem.at[k], rsem.at[k], at(z, x, (y + g + NY) % NY, c))

        def across(yy, k):
            ref = chunk(c, yy)
            send(ref, ref, sib_s.at[k], sib_r.at[k], at(z, x, y, other))

        def first():
            put(0, 0)
            put(1, 0)
            across(y, NY)

        def turn(t):
            for d in range(2):
                if t < steps[d]:
                    g = 1 if d == 0 else -1
                    yy = (y - g * (t + 1) + NY) % NY
                    k = d * (NY // 2) + t
                    arrived(chunk(c, yy), rsem.at[k])
                    if t + 1 < steps[d]:
                        put(d, t + 1)
                    across(yy, k)

        def last():
            arrived(chunk(other, y), sib_r.at[NY])
            for d in range(2):
                g = 1 if d == 0 else -1
                for t in range(steps[d]):
                    arrived(chunk(other, (y - g * (t + 1) + NY) % NY), sib_r.at[d * (NY // 2) + t])

        return first, turn, last

    a_rings = [
        ring(lambda cc, yy, s=s: av.at[cc, s, yy], s, a_s.at[s], a_r.at[s], as_s.at[s], as_r.at[s]) for s in range(2)
    ]
    b_first, b_turn, b_last = ring(lambda cc, yy: w20.at[cc, yy], 0, b_s, b_r, bs_s, bs_r)
    c_first, c_turn, c_last = ring(lambda cc, yy: w21.at[cc, yy], 1, c_s, c_r, cs_s, cs_r)
    for first, _, _ in a_rings:
        first()

    zq = z // 2
    per_half = NZ // 2
    for part, w2 in enumerate((w20, w21)):
        span = SPANS[part]
        for k in range(per_half):
            zz = c * per_half + k
            start = (14 * k) // 3 * 128
            src = av.at[c, start // subw, y, :, pl.ds(start % subw + part * SPANS[0], span)]
            dst = w2.at[z % 2, y, zq]
            copy = pltpu.make_async_remote_copy(
                src_ref=src, dst_ref=dst, send_sem=za_s.at[part, k], recv_sem=za_r.at[part, zq],
                device_id=at(zz, x, y, z % 2), device_id_type=MESH,
            )
            here = pltpu.make_async_copy(src, dst, za_r.at[part, zq])
            remote = jnp.logical_or(zz != z, z % 2 != c)

            @pl.when(remote)
            def _(copy=copy):
                copy.start()

            @pl.when(jnp.logical_not(remote))
            def _(here=here):
                here.start()
            pending.append((copy, remote))
    for dz in range(1, NZ):
        ref = hv.at[z % 2, :, zq]
        send(ref, ref, h_s.at[dz], h_r.at[dz], at((z + dz) % NZ, x, y, c))
    for q in range(NZ // 2):
        arrived(w20.at[c, y, q], za_r.at[0, q])
    b_first()
    for q in range(NZ // 2):
        arrived(w21.at[c, y, q], za_r.at[1, q])
    c_first()

    for t in range(NY // 2):
        for _, turn, _ in a_rings:
            turn(t)
        b_turn(t)
        if t:
            c_turn(t - 1)
    b_last()
    for dz in range(1, NZ):
        zz = (z - dz + NZ) % NZ
        arrived(hv.at[zz % 2, :, zz // 2], h_r.at[dz])

    o_steps = {(d, s): (NZ // 2 if d == s else NZ // 2 - 1) for d in range(2) for s in range(2)}
    owns, dgs, keeps = (own0, own1), (dg0, dg1), []

    def o_send(d, s, t):
        g = 1 if d == 0 else -1
        zz = (z - g * t + NZ) % NZ
        k = (d * 2 + s) * (NZ // 2) + t
        src = owns[s] if t == 0 else dgs[s].at[zz]
        send(src, dgs[s].at[zz], o_s.at[k], o_r.at[k], at((z + g + NZ) % NZ, x, y, c))

    def o_turn(s, t):
        for d in range(2):
            if t < o_steps[d, s]:
                g = 1 if d == 0 else -1
                k = (d * 2 + s) * (NZ // 2) + t
                arrived(dgs[s].at[(z - g * (t + 1) + NZ) % NZ], o_r.at[k])
                if t + 1 < o_steps[d, s]:
                    o_send(d, s, t + 1)

    def down(s):
        w2 = (w20, w21)[s]
        owns[s][...] = mm(hv[...].reshape(-1, 128), w2[...].reshape(-1, SPANS[s]), 0, 0).astype(bf16)
        copy = pltpu.make_async_copy(owns[s], dgs[s].at[z], loc.at[s])
        copy.start()
        keeps.append(copy)
        o_send(0, s, 0)
        o_send(1, s, 0)

    down(0)

    for _, _, last in a_rings:
        last()
    for j in range(8, 28):
        loads[j].wait()
    grad_hidden = mm(av[0, 0].reshape(128, subw), downv[0], 1, 1)
    for j in range(1, 4):
        grad_hidden += mm(av[j // 2, j % 2].reshape(128, subw), downv[j], 1, 1)
    gate_pre = gp[...]
    up_pre = upv[...]
    sig = jax.nn.sigmoid(gate_pre)
    act = gate_pre * sig
    hidden = (act * up_pre).astype(bf16).astype(f32)
    p1[:, :, pl.ds(subw, 128)] = (hidden * grad_hidden).reshape(NY, 16, 128)
    grad_gate = (grad_hidden * up_pre * sig * (1.0 + gate_pre * (1.0 - sig))).astype(bf16)
    grad_up = (grad_hidden * act).astype(bf16)
    both = jnp.concatenate([grad_gate, grad_up], axis=1)
    c_turn(NY // 2 - 1)
    c_last()
    down(1)
    for s in range(4):
        qs[s] = mm(both, guv[other * 4 + s], 1, 1).astype(bf16)
        send(qs.at[s], qr.at[s], q_s.at[s], q_r.at[s], at(z, x, y, other))
    for s in range(4):
        part = mm(both, guv[c * 4 + s], 1, 1)
        (p0, p1)[s // 2][:, :, pl.ds((s % 2) * seg, seg)] = part.reshape(NY, 16, seg)

    pp, sm, rm = (p0, p1), (sm0, sm1), (rm0, rm1)
    m_steps = {(d, s): (NY // 2 if d == s else NY // 2 - 1) for d in range(2) for s in range(2)}

    def m_number(d, t):
        return d * (NY // 2) + t

    def m_send(d, s, t):
        g = 1 if d == 0 else -1
        left = m_steps[d, s] - t
        value = pp[s][(y + g * left + NY) % NY]
        n = m_number(d, t)
        if t:
            value = value + rm[s][m_number(d, t - 1)].astype(f32)
        sm[s][n] = value.astype(bf16)
        send(sm[s].at[n], rm[s].at[n], m_s.at[s * 8 + n], m_r.at[s * 8 + n], at(z, x, (y + g + NY) % NY, c))

    for s in range(4):
        arrived(qr.at[s], q_r.at[s])
        ref = (p0, p1)[s // 2]
        cols = pl.ds((s % 2) * seg, seg)
        ref[:, :, cols] = ref[:, :, cols] + qr[s].astype(f32).reshape(NY, 16, seg)
        if s % 2:
            m_send(0, s // 2, 0)
            m_send(1, s // 2, 0)
    for t in range(NY // 2):
        for s in range(2):
            for d in range(2):
                if t < m_steps[d, s]:
                    n = m_number(d, t)
                    arrived(rm[s].at[n], m_r.at[s * 8 + n])
                    if t + 1 < m_steps[d, s]:
                        m_send(d, s, t + 1)
        o_turn(0, t)
        o_turn(1, t)

    i64 = iota((64, 16), 0)
    k64 = iota((64, 16), 1)
    totals = []
    for s in range(2):
        total = pp[s][y]
        for d in range(2):
            total = total + rm[s][m_number(d, m_steps[d, s] - 1)].astype(f32)
        totals.append(total)
    out = jnp.zeros((64, seg), f32)
    source = (i64 // 8) * CAP + i64 % CAP
    for s in range(4):
        pick = one_hot((source == k64) & ((i64 // CAP) % 4 == s))
        for piece in split(totals[s // 2][:, (s % 2) * seg:(s % 2) * seg + seg]):
            out = out + mm(pick, piece)
    products = jnp.zeros((64, 128), f32)
    pick = one_hot((source == k64) & ((i64 // CAP) % 4 == 0))
    for piece in split(totals[1][:, subw:subw + 128]):
        products = products + mm(pick, piece)
    ys[:, :, :, pl.ds(0, seg)] = out.reshape(NX, 2, 8, seg)
    ys[:, :, :, pl.ds(seg, 128)] = products.reshape(NX, 2, 8, 128)
    keep = pltpu.make_async_copy(ys.at[x, c], yr.at[x, c], y_r.at[x * 2 + c])
    for dx in range(NX):
        for dc in range(2):
            if dx == 0 and dc == 0:
                keep.start()
                continue
            xx, cc = (x + dx) % NX, (c + dc) % 2
            send(ys.at[xx, cc], yr.at[x, c], y_s.at[dx * 2 + dc], y_r.at[x * 2 + c], at(z, xx, y, cc))
    for t in range(NY // 2, NZ // 2):
        o_turn(0, t)
        o_turn(1, t)
    for xx in range(NX):
        for cc in range(2):
            arrived(yr.at[xx, cc], y_r.at[xx * 2 + cc])
    for copy in keeps:
        copy.wait()
    for item in pending:
        if isinstance(item, tuple):
            copy, cond = item

            @pl.when(cond)
            def _(copy=copy):
                copy.wait_send()
        else:
            item.wait_send()


def final_kernel(
    logits_ref, group_ref, member_ref, yr_ref, dg0, dg1, token_out, logit_ref, down_out, stage, in0, in1, sems, down_sems
):
    seg = stage.shape[2]
    per_half = NZ // 2
    copies = []
    fetch = [pltpu.make_async_copy(dg0, in0, sems.at[8]), pltpu.make_async_copy(dg1, in1, sems.at[9])]
    for copy in fetch:
        copy.start()
    affinity, affinity_sum, hits, slot8, gate8 = routing(logits_ref[...], group_ref[...], member_ref[...])
    grads = yr_ref[:, :, :, 0:seg].reshape(64, seg)
    pieces = jnp.concatenate(split(grads), axis=0)
    expand = expand_rows(64)
    place = mm(slot8.astype(bf16), expand, 0, 1)
    colseg = (iota((128, 64), 1) // CAP) % 8
    for j in range(8):
        chosen = jnp.where(colseg == j, place, 0.0).astype(bf16)
        stage[j] = mm(jnp.concatenate([chosen] * 3, axis=1), pieces).astype(bf16)
        copy = pltpu.make_async_copy(stage.at[j], token_out.at[:, pl.ds(j * seg, seg)], sems.at[j])
        copy.start()
        copies.append(copy)
    for s, part in enumerate((in0, in1)):
        fetch[s].wait()
        for zz in range(NZ):
            k = zz % per_half
            start = (14 * k) // 3
            end = (14 * (k + 1)) // 3
            low = start * 128 + s * SPANS[0]
            width = min(SPANS[s], end * 128 - low)
            copy = pltpu.make_async_copy(
                part.at[zz, :, pl.ds(0, width)],
                down_out.at[:, pl.ds((zz // per_half) * 4 * seg + low, width)],
                down_sems.at[zz * 2 + s],
            )
            copy.start()
            copies.append(copy)
    products = yr_ref[:, :, :, seg:seg + 128].reshape(64, 128)
    folded = jnp.zeros((8, 128), f32)
    for piece in split(products):
        folded = folded + mm(expand, piece, 0, 0)
    router = jnp.sum(folded, axis=1, keepdims=True)
    used = slot8 > 0.0
    routes = jnp.where(used, router / jnp.where(used, gate8, 1.0), 0.0)
    row = iota(slot8.shape, 0)
    route_grad = jnp.zeros(slot8.shape, f32)
    for w in range(EXPERTS):
        window_grad = jnp.sum(jnp.where((row // CAP) == w, routes, 0.0), axis=0, keepdims=True)
        route_grad = jnp.where(hits[w], window_grad, route_grad)
    mean = jnp.sum(route_grad * affinity, axis=0, keepdims=True) / affinity_sum
    logit_ref[...] = affinity * (1.0 - affinity) * route_scale / affinity_sum * (route_grad - mean)
    for copy in copies:
        copy.wait()


def body(cotangent, logits, group_pick, member_pick, saved_gate, saved_up, gate_weight, up_weight, down_weight):
    tokens, width = cotangent.shape
    seg = width // 8
    subw = 2 * seg
    vmem = pl.BlockSpec(memory_space=pltpu.VMEM)
    hbm = pl.BlockSpec(memory_space=pl.ANY)
    logits_t, group_t, member_t = logits.T, group_pick.T, member_pick.T
    dma = pltpu.SemaphoreType.DMA
    scratch = [
        pltpu.VMEM((8, tokens, seg), bf16),
        pltpu.VMEM((4, 128, subw), bf16),
        pltpu.VMEM((8, seg, 256), bf16),
        pltpu.VMEM((NX, 2, 8, seg), f32),
        pltpu.VMEM((NX, 2, 8, seg), f32),
        pltpu.VMEM((2, 2, NY, 16, subw), bf16),
        pltpu.VMEM((2, NY, NZ // 2, 16, SPANS[0]), bf16),
        pltpu.VMEM((2, NY, NZ // 2, 16, SPANS[1]), bf16),
        pltpu.VMEM((2, NY, NZ // 2, 16, 128), bf16),
        pltpu.VMEM((128, 128), f32),
        pltpu.VMEM((128, 128), f32),
        pltpu.VMEM((128, SPANS[0]), bf16),
        pltpu.VMEM((128, SPANS[1]), bf16),
        pltpu.VMEM((4, 128, seg), bf16),
        pltpu.VMEM((4, 128, seg), bf16),
        pltpu.VMEM((NY, 16, subw), f32),
        pltpu.VMEM((NY, 16, subw + 128), f32),
        pltpu.VMEM((8, 16, subw), bf16),
        pltpu.VMEM((8, 16, subw + 128), bf16),
        pltpu.VMEM((8, 16, subw), bf16),
        pltpu.VMEM((8, 16, subw + 128), bf16),
        pltpu.VMEM((NX, 2, 8, seg + 128), f32),
        dma((28,)),
        dma((8,)), dma((8,)),
        dma((2, 6)), dma((2, 6)),
        dma((2, 8)), dma((2, 8)), dma((2, 9)), dma((2, 9)),
        dma((8,)), dma((8,)), dma((9,)), dma((9,)),
        dma((8,)), dma((8,)), dma((9,)), dma((9,)),
        dma((12,)), dma((12,)),
        dma((24,)), dma((24,)),
        dma((4,)), dma((4,)),
        dma((16,)), dma((16,)),
        dma((8,)), dma((8,)),
        dma((2,)),
    ]
    yr, dg0, dg1 = pl.pallas_call(
        main_kernel,
        out_shape=(
            jax.ShapeDtypeStruct((NX, 2, 8, seg + 128), f32),
            jax.ShapeDtypeStruct((NZ, 128, SPANS[0]), bf16),
            jax.ShapeDtypeStruct((NZ, 128, SPANS[1]), bf16),
        ),
        in_specs=[vmem] * 5 + [hbm] * 4,
        out_specs=(hbm, hbm, hbm),
        scratch_shapes=scratch,
        compiler_params=pltpu.CompilerParams(
            collective_id=0, has_side_effects=True, vmem_limit_bytes=62 * 1024 * 1024
        ),
    )(logits_t, group_t, member_t, saved_gate, saved_up, cotangent, gate_weight, up_weight, down_weight)
    token_grad, logit_grad, down_grad = pl.pallas_call(
        final_kernel,
        out_shape=(
            jax.ShapeDtypeStruct((tokens, width), bf16),
            jax.ShapeDtypeStruct((8, tokens), f32),
            jax.ShapeDtypeStruct((128, width), bf16),
        ),
        in_specs=[vmem] * 4 + [hbm] * 2,
        out_specs=(hbm, vmem, hbm),
        scratch_shapes=[
            pltpu.VMEM((8, tokens, seg), bf16),
            pltpu.VMEM((NZ, 128, SPANS[0]), bf16),
            pltpu.VMEM((NZ, 128, SPANS[1]), bf16),
            dma((10,)),
            dma((24,)),
        ],
        compiler_params=pltpu.CompilerParams(vmem_limit_bytes=62 * 1024 * 1024),
    )(logits_t, group_t, member_t, yr, dg0, dg1)
    return token_grad, logit_grad.T, down_grad


def solution(mesh):
    placed = (
        P(("dp", "expert"), None),
        P(("dp", "expert"), None),
        P(("dp", "expert"), None),
        P(("dp", "expert"), None),
        P("dp", "expert"),
        P("dp", "expert"),
        P(None, "expert"),
        P(None, "expert"),
        P("expert", None),
    )
    return jax.shard_map(
        body,
        mesh=mesh,
        in_specs=placed,
        out_specs=(P(("dp", "expert"), None), P(("dp", "expert"), None), P("expert", None)),
        check_vma=False,
    )
```

```python
import functools

import jax
import jax.numpy as jnp
from jax import lax
from jax.experimental import pallas as pl
from jax.experimental.pallas import tpu as pltpu
from jax.sharding import PartitionSpec as P

EXPERTS = 4
CAP = 2
GROUP_SIZE = 32
STRIDE = 64
route_scale = 2.5
MESH = pl.DeviceIdType.MESH
bf16 = jnp.bfloat16
f32 = jnp.float32

NX = EXPERTS
NY = 8
NZ = 12
SPAN = 640
TILES = SPAN // 128


def iota(shape, dim):
    return lax.broadcasted_iota(jnp.int32, shape, dim)


def one_hot(mask):
    return jnp.where(mask, 1.0, 0.0).astype(bf16)


def mm(a, b, ca=1, cb=0):
    return lax.dot_general(a, b, (((ca,), (cb,)), ((), ())), preferred_element_type=f32)


def split(v):
    hi = v.astype(bf16)
    rest = v - hi.astype(f32)
    mid = rest.astype(bf16)
    low = (rest - mid.astype(f32)).astype(bf16)
    return hi, mid, low


def routing(logits, group, member):
    chosen = group * GROUP_SIZE + member
    affinity = jax.nn.sigmoid(logits)
    affinity_sum = jnp.sum(affinity, axis=0, keepdims=True)
    gate = (route_scale * affinity / affinity_sum).astype(bf16).astype(f32)
    row = iota(chosen.shape, 0)
    hits = [chosen == w * STRIDE for w in range(EXPERTS)]
    member8 = jnp.zeros(chosen.shape, f32)
    gate8 = jnp.zeros(chosen.shape, f32)
    for w in range(EXPERTS):
        in_window = jnp.sum(jnp.where(hits[w], 1.0, 0.0), axis=0, keepdims=True)
        window_gate = jnp.sum(jnp.where(hits[w], gate, 0.0), axis=0, keepdims=True)
        mine = (row // CAP) == w
        member8 = jnp.where(mine, in_window, member8)
        gate8 = jnp.where(mine, window_gate, gate8)
    tokens = chosen.shape[1]
    before = one_hot(iota((tokens, tokens), 0) < iota((tokens, tokens), 1))
    earlier = mm(member8.astype(bf16), before)
    slot8 = jnp.where(earlier == (row % CAP).astype(f32), member8, 0.0)
    return affinity, affinity_sum, hits, slot8, gate8


def expand_rows(rows):
    i = iota((rows, EXPERTS * CAP), 0)
    j = iota((rows, EXPERTS * CAP), 1)
    per = rows // EXPERTS
    return one_hot((i // per) * CAP + i % CAP == j)


def main_kernel(
    logits_ref, group_ref, member_ref, sg_ref, su_ref, cot_hbm, gate_hbm, up_hbm, down_hbm,
    yr, dg,
    cotv, downv, guv, xs, xr, av, w2, hv, gp, upv, ov, qs, qr, p0, p1, p2, p3,
    sm0, sm1, sm2, sm3, rm0, rm1, rm2, rm3, ys,
    load_sem,
    xs_s, xs_r, za_s, za_r, a_s, a_r, as_s, as_r, b_s, b_r, bs_s, bs_r, h_s, h_r, o_s, o_r,
    q_s, q_r, m_s, m_r, y_s, y_r, loc,
):
    e = lax.axis_index("expert")
    z = lax.axis_index("dp")
    x = e // (2 * NY)
    y = (e // 2) % NY
    c = e % 2
    other = 1 - c
    half = cotv.shape[0] // 2
    seg = cotv.shape[2]
    subw = seg * 2
    pending = []

    def at(zz, xx, yy, cc):
        return (zz, (xx * NY + yy) * 2 + cc)

    def send(src, dst, ssem, rsem, dev):
        copy = pltpu.make_async_remote_copy(
            src_ref=src, dst_ref=dst, send_sem=ssem, recv_sem=rsem, device_id=dev, device_id_type=MESH
        )
        copy.start()
        pending.append(copy)

    def arrived(dst, rsem):
        pltpu.make_async_remote_copy(
            src_ref=dst, dst_ref=dst, send_sem=rsem, recv_sem=rsem,
            device_id=at(z, x, y, other), device_id_type=MESH,
        ).wait_recv()

    loads = []

    def load(src, dst, k):
        copy = pltpu.make_async_copy(src, dst, load_sem.at[k])
        copy.start()
        loads.append(copy)

    for j in range(8):
        load(cot_hbm.at[:, pl.ds(j * seg, seg)], cotv.at[j], j)
    barrier = pltpu.get_barrier_semaphore()
    greeted = 0

    def greet(dev):
        pl.semaphore_signal(barrier, inc=1, device_id=dev, device_id_type=MESH)

    for dz in range(NZ):
        for dc in range(2):
            if dz or dc:
                greet(at((z + dz) % NZ, x, y, (c + dc) % 2))
                greeted += 1
    for dx in range(1, NX):
        for dc in range(2):
            greet(at(z, (x + dx) % NX, y, (c + dc) % 2))
            greeted += 1
    for dy in (1, NY - 1):
        greet(at(z, x, (y + dy) % NY, c))
        greeted += 1

    def own_hidden():
        i = iota((128, 128), 0)
        k = iota((128, 128), 1)
        perm = one_hot(k == ((i // 4) % NX) * (4 * NY) + (i // (4 * NX)) * 4 + i % 4)
        gp[...] = mm(perm, sg_ref[...])
        upv[...] = mm(perm, su_ref[...])
        gate_pre = gp[...]
        hidden = (gate_pre * jax.nn.sigmoid(gate_pre) * upv[...]).astype(bf16)
        zz = z // 2
        hv[z % 2, :, zz] = hidden.reshape(NY, 16, 128)

    affinity, affinity_sum, hits, slot8, gate8 = routing(logits_ref[...], group_ref[...], member_ref[...])
    rows64 = mm(expand_rows(64), (slot8 * gate8).astype(bf16))
    rowseg = (iota((64, 128), 0) // CAP) % 8
    spread = jnp.concatenate(
        [jnp.where(rowseg == j, rows64, 0.0).astype(bf16) for j in range(8)], axis=1
    )
    for j in range(8):
        loads[j].wait()
    gated = mm(spread, cotv[...].reshape(8 * 128, seg))
    xs[...] = gated.reshape(NX, 2, 8, seg)

    pl.semaphore_wait(barrier, greeted)

    keep = pltpu.make_async_copy(xs.at[x, c], xr.at[x, c], xs_r.at[x * 2 + c])
    for dx in (2, 1, 3, 0):
        for dc in range(2):
            if dx == 0 and dc == 0:
                keep.start()
                continue
            xx, cc = (x + dx) % NX, (c + dc) % 2
            send(xs.at[xx, cc], xr.at[x, c], xs_s.at[dx * 2 + dc], xs_r.at[x * 2 + c], at(z, xx, y, cc))
    for j in range(4):
        load(down_hbm.at[:, pl.ds(j * subw, subw)], downv.at[j], 8 + j)
    for j in range(8):
        load(gate_hbm.at[pl.ds(j * seg, seg), :], guv.at[j, :, pl.ds(0, 128)], 12 + j)
        load(up_hbm.at[pl.ds(j * seg, seg), :], guv.at[j, :, pl.ds(128, 128)], 20 + j)
    own_hidden()

    def h_send(d, t):
        g = 1 if d == 0 else -1
        zz = (z - g * t + NZ) % NZ
        ref = hv.at[zz % 2, :, zz // 2]
        k = d * (NZ // 2) + t
        send(ref, ref, h_s.at[k], h_r.at[k], at((z + g + NZ) % NZ, x, y, c))

    def h_turn(t):
        for d in range(2):
            if t < NZ // 2 - d:
                g = 1 if d == 0 else -1
                zz = (z - g * (t + 1) + NZ) % NZ
                arrived(hv.at[zz % 2, :, zz // 2], h_r.at[d * (NZ // 2) + t])
                if t + 1 < NZ // 2 - d:
                    h_send(d, t + 1)

    h_send(0, 0)
    h_send(1, 0)
    h_turn(0)
    for xx in range(NX):
        for cc in range(2):
            arrived(xr.at[xx, cc], xs_r.at[xx * 2 + cc])
    i16 = iota((16, 64), 0)
    k16 = iota((16, 64), 1)
    got = xr[...].reshape(64, seg).astype(bf16)
    for s in range(4):
        pick = one_hot(((k16 // 8) * CAP + k16 % CAP == i16) & ((k16 // CAP) % 4 == s))
        av[c, s // 2, y, :, pl.ds((s % 2) * seg, seg)] = mm(pick, got).astype(bf16)

    def ring(chunk, longer, ssem, rsem):
        steps = [NY // 2 if d == longer else NY // 2 - 1 for d in range(2)]

        def put(d, t):
            g = 1 if d == 0 else -1
            ref = chunk((y - g * t + NY) % NY)
            k = d * (NY // 2) + t
            send(ref, ref, ssem.at[k], rsem.at[k], at(z, x, (y + g + NY) % NY, c))

        def turn(d, t):
            if t < steps[d]:
                g = 1 if d == 0 else -1
                arrived(chunk((y - g * (t + 1) + NY) % NY), rsem.at[d * (NY // 2) + t])
                if t + 1 < steps[d]:
                    put(d, t + 1)

        return put, turn

    def whose(d, t):
        return (y - (1 if d == 0 else -1) * (t + 1) + NY) % NY

    a_rings = [ring(lambda yy, s=s: av.at[c, s, yy], s, a_s.at[s], a_r.at[s]) for s in range(2)]

    def a_across(s, yy, k):
        ref = av.at[c, s, yy]
        send(ref, ref, as_s.at[s, k], as_r.at[s, k], at(z, x, y, other))

    def a_turn(t):
        for s in range(2):
            for d in range(2):
                a_rings[s][1](d, t)
                if t < NY // 2 - (d != s):
                    a_across(s, whose(d, t), d * (NY // 2) + t)

    for put, _ in a_rings:
        put(0, 0)
        put(1, 0)
    for s in range(2):
        a_across(s, y, NY)

    zq = z // 2
    per_half = NZ // 2
    for k in range(per_half):
        zz = c * per_half + k
        start = (14 * k) // 3 * 128
        src = av.at[c, start // subw, y, :, pl.ds(start % subw, SPAN)]
        dst = w2.at[z % 2, y, zq]
        copy = pltpu.make_async_remote_copy(
            src_ref=src, dst_ref=dst, send_sem=za_s.at[k], recv_sem=za_r.at[zq],
            device_id=at(zz, x, y, z % 2), device_id_type=MESH,
        )
        here = pltpu.make_async_copy(src, dst, za_r.at[zq])
        remote = jnp.logical_or(zz != z, z % 2 != c)

        @pl.when(remote)
        def _(copy=copy):
            copy.start()

        @pl.when(jnp.logical_not(remote))
        def _(here=here):
            here.start()
        pending.append((copy, remote))
    h_turn(1)
    a_turn(0)
    h_turn(2)

    b_rings = []
    order = (0, 1, -1, 2, -2, 3)
    for n, r in enumerate(order):
        q = (zq + r + NZ // 2) % (NZ // 2)
        put, turn = ring(lambda yy, q=q: w2.at[c, yy, q], n % 2, b_s.at[n], b_r.at[n])
        b_rings.append((put, turn))
        arrived(w2.at[c, y, q], za_r.at[q])
        put(0, 0)
        put(1, 0)

    def b_across(yy, k):
        ref = w2.at[c, yy]
        send(ref, ref, bs_s.at[k], bs_r.at[k], at(z, x, y, other))

    b_across(y, NY)

    def b_turn(t):
        for _, turn in b_rings:
            for d in range(2):
                turn(d, t)
        if t < NY // 2 - 1:
            for d in range(2):
                b_across(whose(d, t), d * (NY // 2) + t)
        else:
            b_across(whose(0, t), t)

    h_turn(3)
    a_turn(1)
    b_turn(0)
    h_turn(4)
    a_turn(2)
    b_turn(1)
    h_turn(5)
    a_turn(3)
    b_turn(2)

    for s in range(2):
        arrived(av.at[other, s, y], as_r.at[s, NY])
        for d in range(2):
            for t in range(NY // 2 - (d != s)):
                arrived(av.at[other, s, whose(d, t)], as_r.at[s, d * (NY // 2) + t])
    for j in range(8, 28):
        loads[j].wait()
    grad_hidden = mm(av[0, 0].reshape(128, subw), downv[0], 1, 1)
    for j in range(1, 4):
        grad_hidden += mm(av[j // 2, j % 2].reshape(128, subw), downv[j], 1, 1)
    gate_pre = gp[...]
    up_pre = upv[...]
    sig = jax.nn.sigmoid(gate_pre)
    act = gate_pre * sig
    hidden = (act * up_pre).astype(bf16).astype(f32)
    p3[:, :, pl.ds(seg, 128)] = (hidden * grad_hidden).reshape(NY, 16, 128)
    grad_gate = (grad_hidden * up_pre * sig * (1.0 + gate_pre * (1.0 - sig))).astype(bf16)
    grad_up = (grad_hidden * act).astype(bf16)
    both = jnp.concatenate([grad_gate, grad_up], axis=1)
    for s in range(4):
        qs[s] = mm(both, guv[other * 4 + s], 1, 1).astype(bf16)
        send(qs.at[s], qr.at[s], q_s.at[s], q_r.at[s], at(z, x, y, other))
    b_turn(3)
    pp, sm, rm = (p0, p1, p2, p3), (sm0, sm1, sm2, sm3), (rm0, rm1, rm2, rm3)
    for s in range(4):
        pp[s][:, :, pl.ds(0, seg)] = mm(both, guv[c * 4 + s], 1, 1).reshape(NY, 16, seg)

    arrived(w2.at[other, y], bs_r.at[NY])
    for d in range(2):
        for t in range(NY // 2 - d):
            arrived(w2.at[other, whose(d, t)], bs_r.at[d * (NY // 2) + t])
    keeps = []

    def o_place(zz, p):
        low = (zz // per_half) * (4 * seg) + (14 * (zz % per_half)) // 3 * 128 + p * 128
        return dg.at[:, pl.ds(pl.multiple_of(low, 128), 128)]

    def o_when(zz, p, f):
        if p < TILES - 1:
            f()
        else:
            pl.when(zz % 3 != 0)(f)

    def o_long(d, p):
        return NZ // 2 - (d != p % 2)

    def o_keep(zz, p, k):
        copy = pltpu.make_async_copy(ov.at[zz, p], o_place(zz, p), loc.at[k])
        o_when(zz, p, copy.start)
        keeps.append((copy, zz, p))

    def o_send(d, p, t):
        g = 1 if d == 0 else -1
        zz = (z - g * t + NZ) % NZ
        k = d * (NZ // 2) + t
        ref = ov.at[zz, p]
        copy = pltpu.make_async_remote_copy(
            src_ref=ref, dst_ref=ref, send_sem=o_s.at[p, k], recv_sem=o_r.at[p, k],
            device_id=at((z + g + NZ) % NZ, x, y, c), device_id_type=MESH,
        )
        o_when(zz, p, copy.start)
        sent.append((copy, zz, p))

    def o_turn(t):
        for p in range(TILES):
            for d in range(2):
                if t < o_long(d, p):
                    g = 1 if d == 0 else -1
                    zz = (z - g * (t + 1) + NZ) % NZ
                    k = d * (NZ // 2) + t
                    o_when(zz, p, lambda: arrived(ov.at[zz, p], o_r.at[p, k]))
                    if t + 1 < o_long(d, p):
                        o_send(d, p, t + 1)
                    o_keep(zz, p, p * (NZ + 1) + k)

    sent = []
    mine = mm(hv[...].reshape(-1, 128), w2[...].reshape(-1, SPAN), 0, 0).astype(bf16)
    for p in range(TILES):
        ov[z, p] = mine[:, p * 128:p * 128 + 128]
        o_send(0, p, 0)
        o_send(1, p, 0)
        o_keep(z, p, p * (NZ + 1) + NZ)

    m_steps = {(d, s): (NY // 2 if d == s % 2 else NY // 2 - 1) for d in range(2) for s in range(4)}

    def m_number(d, t):
        return d * (NY // 2) + t

    def m_send(d, s, t):
        g = 1 if d == 0 else -1
        left = m_steps[d, s] - t
        value = pp[s][(y + g * left + NY) % NY]
        n = m_number(d, t)
        if t:
            value = value + rm[s][m_number(d, t - 1)].astype(f32)
        sm[s][n] = value.astype(bf16)
        send(sm[s].at[n], rm[s].at[n], m_s.at[s * 8 + n], m_r.at[s * 8 + n], at(z, x, (y + g + NY) % NY, c))

    for s in range(4):
        arrived(qr.at[s], q_r.at[s])
        ref = pp[s]
        ref[:, :, pl.ds(0, seg)] = ref[:, :, pl.ds(0, seg)] + qr[s].astype(f32).reshape(NY, 16, seg)
        m_send(0, s, 0)
        m_send(1, s, 0)
    for t in range(NY // 2):
        o_turn(t)
        for s in range(4):
            for d in range(2):
                if t < m_steps[d, s]:
                    n = m_number(d, t)
                    arrived(rm[s].at[n], m_r.at[s * 8 + n])
                    if t + 1 < m_steps[d, s]:
                        m_send(d, s, t + 1)

    i64 = iota((64, 16), 0)
    k64 = iota((64, 16), 1)
    out = jnp.zeros((64, seg), f32)
    source = (i64 // 8) * CAP + i64 % CAP
    for s in range(4):
        total = pp[s][y]
        for d in range(2):
            total = total + rm[s][m_number(d, m_steps[d, s] - 1)].astype(f32)
        pick = one_hot((source == k64) & ((i64 // CAP) % 4 == s))
        for piece in split(total[:, 0:seg]):
            out = out + mm(pick, piece)
    products = jnp.zeros((64, 128), f32)
    pick = one_hot((source == k64) & ((i64 // CAP) % 4 == 0))
    for piece in split(total[:, seg:seg + 128]):
        products = products + mm(pick, piece)
    ys[:, :, :, pl.ds(0, seg)] = out.reshape(NX, 2, 8, seg)
    ys[:, :, :, pl.ds(seg, 128)] = products.reshape(NX, 2, 8, 128)
    keep = pltpu.make_async_copy(ys.at[x, c], yr.at[x, c], y_r.at[x * 2 + c])
    for dx in (2, 1, 3, 0):
        for dc in range(2):
            if dx == 0 and dc == 0:
                keep.start()
                continue
            xx, cc = (x + dx) % NX, (c + dc) % 2
            send(ys.at[xx, cc], yr.at[x, c], y_s.at[dx * 2 + dc], y_r.at[x * 2 + c], at(z, xx, y, cc))
    for t in range(NY // 2, NZ // 2):
        o_turn(t)
    for xx in range(NX):
        for cc in range(2):
            arrived(yr.at[xx, cc], y_r.at[xx * 2 + cc])
    for copy, zz, p in keeps:
        o_when(zz, p, copy.wait)
    for copy, zz, p in sent:
        o_when(zz, p, copy.wait_send)
    for item in pending:
        if isinstance(item, tuple):
            copy, cond = item

            @pl.when(cond)
            def _(copy=copy):
                copy.wait_send()
        else:
            item.wait_send()


def final_kernel(
    logits_ref, group_ref, member_ref, yr_ref, dg, token_out, logit_ref, down_out, stage, whole, sems
):
    seg = stage.shape[2]
    copies = []
    fetch = pltpu.make_async_copy(dg, whole, sems.at[8])
    fetch.start()
    affinity, affinity_sum, hits, slot8, gate8 = routing(logits_ref[...], group_ref[...], member_ref[...])
    grads = yr_ref[:, :, :, 0:seg].reshape(64, seg)
    pieces = jnp.concatenate(split(grads), axis=0)
    expand = expand_rows(64)
    place = mm(slot8.astype(bf16), expand, 0, 1)
    colseg = (iota((128, 64), 1) // CAP) % 8
    for j in range(8):
        chosen = jnp.where(colseg == j, place, 0.0).astype(bf16)
        stage[j] = mm(jnp.concatenate([chosen] * 3, axis=1), pieces).astype(bf16)
        copy = pltpu.make_async_copy(stage.at[j], token_out.at[:, pl.ds(j * seg, seg)], sems.at[j])
        copy.start()
        copies.append(copy)
    fetch.wait()
    copy = pltpu.make_async_copy(whole, down_out, sems.at[9])
    copy.start()
    copies.append(copy)
    products = yr_ref[:, :, :, seg:seg + 128].reshape(64, 128)
    folded = jnp.zeros((8, 128), f32)
    for piece in split(products):
        folded = folded + mm(expand, piece, 0, 0)
    router = jnp.sum(folded, axis=1, keepdims=True)
    used = slot8 > 0.0
    routes = jnp.where(used, router / jnp.where(used, gate8, 1.0), 0.0)
    row = iota(slot8.shape, 0)
    route_grad = jnp.zeros(slot8.shape, f32)
    for w in range(EXPERTS):
        window_grad = jnp.sum(jnp.where((row // CAP) == w, routes, 0.0), axis=0, keepdims=True)
        route_grad = jnp.where(hits[w], window_grad, route_grad)
    mean = jnp.sum(route_grad * affinity, axis=0, keepdims=True) / affinity_sum
    logit_ref[...] = affinity * (1.0 - affinity) * route_scale / affinity_sum * (route_grad - mean)
    for copy in copies:
        copy.wait()


def body(cotangent, logits, group_pick, member_pick, saved_gate, saved_up, gate_weight, up_weight, down_weight):
    tokens, width = cotangent.shape
    seg = width // 8
    subw = 2 * seg
    vmem = pl.BlockSpec(memory_space=pltpu.VMEM)
    hbm = pl.BlockSpec(memory_space=pl.ANY)
    logits_t, group_t, member_t = logits.T, group_pick.T, member_pick.T
    dma = pltpu.SemaphoreType.DMA
    scratch = [
        pltpu.VMEM((8, tokens, seg), bf16),
        pltpu.VMEM((4, 128, subw), bf16),
        pltpu.VMEM((8, seg, 256), bf16),
        pltpu.VMEM((NX, 2, 8, seg), f32),
        pltpu.VMEM((NX, 2, 8, seg), f32),
        pltpu.VMEM((2, 2, NY, 16, subw), bf16),
        pltpu.VMEM((2, NY, NZ // 2, 16, SPAN), bf16),
        pltpu.VMEM((2, NY, NZ // 2, 16, 128), bf16),
        pltpu.VMEM((128, 128), f32),
        pltpu.VMEM((128, 128), f32),
        pltpu.VMEM((NZ, TILES, 128, 128), bf16),
        pltpu.VMEM((4, 128, seg), bf16),
        pltpu.VMEM((4, 128, seg), bf16),
    ]
    widths = (seg, seg, seg, seg + 128)
    scratch += [pltpu.VMEM((NY, 16, w), f32) for w in widths]
    scratch += [pltpu.VMEM((8, 16, w), bf16) for w in widths * 2]
    scratch += [
        pltpu.VMEM((NX, 2, 8, seg + 128), f32),
        dma((28,)),
        dma((8,)), dma((8,)),
        dma((6,)), dma((6,)),
        dma((2, 8)), dma((2, 8)), dma((2, 9)), dma((2, 9)),
        dma((6, 8)), dma((6, 8)), dma((9,)), dma((9,)),
        dma((12,)), dma((12,)),
        dma((TILES, 12)), dma((TILES, 12)),
        dma((4,)), dma((4,)),
        dma((32,)), dma((32,)),
        dma((8,)), dma((8,)),
        dma((TILES * (NZ + 1),)),
    ]
    yr, dg = pl.pallas_call(
        main_kernel,
        out_shape=(
            jax.ShapeDtypeStruct((NX, 2, 8, seg + 128), f32),
            jax.ShapeDtypeStruct((128, width), bf16),
        ),
        in_specs=[vmem] * 5 + [hbm] * 4,
        out_specs=(hbm, hbm),
        scratch_shapes=scratch,
        compiler_params=pltpu.CompilerParams(
            collective_id=0, has_side_effects=True, vmem_limit_bytes=62 * 1024 * 1024
        ),
    )(logits_t, group_t, member_t, saved_gate, saved_up, cotangent, gate_weight, up_weight, down_weight)
    token_grad, logit_grad, down_grad = pl.pallas_call(
        final_kernel,
        out_shape=(
            jax.ShapeDtypeStruct((tokens, width), bf16),
            jax.ShapeDtypeStruct((8, tokens), f32),
            jax.ShapeDtypeStruct((128, width), bf16),
        ),
        in_specs=[vmem] * 4 + [hbm],
        out_specs=(hbm, vmem, hbm),
        scratch_shapes=[
            pltpu.VMEM((8, tokens, seg), bf16),
            pltpu.VMEM((128, width), bf16),
            dma((10,)),
        ],
        compiler_params=pltpu.CompilerParams(vmem_limit_bytes=62 * 1024 * 1024),
    )(logits_t, group_t, member_t, yr, dg)
    return token_grad, logit_grad.T, down_grad


def solution(mesh):
    placed = (
        P(("dp", "expert"), None),
        P(("dp", "expert"), None),
        P(("dp", "expert"), None),
        P(("dp", "expert"), None),
        P("dp", "expert"),
        P("dp", "expert"),
        P(None, "expert"),
        P(None, "expert"),
        P("expert", None),
    )
    return jax.shard_map(
        body,
        mesh=mesh,
        in_specs=placed,
        out_specs=(P(("dp", "expert"), None), P(("dp", "expert"), None), P("expert", None)),
        check_vma=False,
    )
```
